256 devices in a mesh: exp: 4 (over z_lo), inner: 4 (over z_hi, core), outer: 16 (over x, y).
Axes of the slice: x: 4, y: 4, z: 8 (z_hi: 2, z_lo: 4; z = z_hi * 4 + z_lo), core: 2. Of those that a mesh axis runs over, the one named last changes fastest.
Arguments:
- activations: bfloat16 [262144, 2048], P(('exp', 'inner', 'outer')), parts along dimension 0, may hold values from -6 to 6
- cotangent: bfloat16 [262144, 768], P(('exp', 'inner', 'outer')), parts along dimension 0, may hold values from -0.0625 to 0.0625
- tile_rows: int32 [2048], P(('exp', 'inner', 'outer')), parts along dimension 0, may hold values from 1 to 128, as said below
- params: bfloat16 [8192, 768], P(('exp', 'inner')), parts along dimension 0, may hold values from -5 to 5
- first_moment: float32 [8192, 768], P(('exp', 'inner')), parts along dimension 0, may hold values from -0.6 to 0.6
- second_moment: float32 [8192, 768], P(('exp', 'inner')), parts along dimension 0, may hold values from 0.005 to 0.05
Outputs:
- new_params: bfloat16 [8192, 768], P('exp'), parts along dimension 0
- first_new: float32 [8192, 768], P(('exp', 'inner', 'outer')), parts along dimension 0
- second_new: float32 [8192, 768], P(('exp', 'inner', 'outer')), parts along dimension 0
The draws below stay inside these ranges and needn't reach their ends.
There are 4 independent parts, one for each index of `exp`. The reference program is written for one: setup_inputs(seed, part) draws one part's arguments, and reference() takes and returns one part's arrays. A program takes and returns all parts, laid end to end along the dimension named above; each array names one. Nothing has to cross between parts.
Inputs may be any that keep to these rules, and one draw needn't show every extreme that they name: In each tile the live rows are the first tile_rows[t] rows.
All inputs are finite; a program needn't handle non-finite values.
Results may differ from the reference program's by a relative error of at most 0.001.
Values may be sent and summed in bfloat16 or wider, within the bound.
A program may use at most 64 MiB of HBM per device.

```python
import math
import jax
import jax.numpy as jnp
from jax import lax

D = 2048
F = 768
TILE = 128
TOK_DEV = 1024
TOKENS = 65536


def draw_tile_rows(key, part):
    key = jax.random.fold_in(key, 11)
    count = TOKENS // TILE
    first_key, second_key, third_key = jax.random.split(key, 3)
    values = jax.random.randint(first_key, (count,), 1, TILE + 1)
    full_at = jax.random.randint(second_key, (), 0, count)
    offset = jax.random.randint(third_key, (), 1, count)
    single_at = (full_at + offset) % count
    positions = lax.broadcasted_iota(jnp.int32, (count,), 0)
    values = jnp.where(positions == full_at, TILE, values)
    values = jnp.where(positions == single_at, 1, values)
    return values.astype(jnp.int32)


def spiked(array, rng, source, target, blocks, factor):
    def block_of(position):
        return (jnp.arange(array.shape[position]) // (array.shape[position] // blocks)).reshape((-1,) + (1,) * (array.ndim - 1 - position))

    one_side = jax.random.permutation(rng, blocks)[block_of(target)]
    far = (block_of(target) + blocks // 2) % blocks
    return jnp.where((block_of(source) == one_side) | (block_of(source) == far), factor * array, array)


def steps_of(key, extent, cuts, low, largest):
    factor_of = 1.0
    for axis_at, blocks in cuts:
        steps = jax.random.uniform(jax.random.fold_in(jax.random.fold_in(key, 6), axis_at), (blocks,), jnp.float32, low / len(cuts), largest / len(cuts))
        factor_of = factor_of * jnp.repeat(jnp.exp(steps), extent[axis_at] // blocks).reshape((-1,) + (1,) * (len(extent) - 1 - axis_at))
    return factor_of


def scatter_about(key, dims, width, bound, pieces=(), kind=jnp.bfloat16):
    entries = jax.random.normal(key, dims, jnp.float32) * width
    if len(pieces) > 0:
        entries = steps_of(key, dims, pieces, -0.22, 0.18) * entries
    return jnp.clip(entries, min=-bound, max=bound).astype(kind)


def bell_draw_with(key, extent, spread, reach, shards, heavy, dtype=jnp.bfloat16):
    drawn = spread * jax.random.normal(key, extent, jnp.float32)
    if shards:
        drawn = drawn * steps_of(key, extent, shards, -0.22, 0.18)
    return jnp.clip(spiked(drawn, jax.random.fold_in(key, 3), *heavy), -reach, reach).astype(dtype)


def setup_inputs(seed: int = 0, part: int = 0) -> dict:
    splits = jax.random.split(jax.random.key(seed), 7)
    part_splits = jax.random.split(jax.random.fold_in(splits[6], part), 7)
    return {
        "activations": scatter_about(part_splits[0], (TOKENS, D), 1.0, 6.0, ((0, 64),)),
        "cotangent": bell_draw_with(part_splits[1], (TOKENS, F), (TOKENS ** -0.5), 0.0625, ((0, 64),), (0, 1, 64, 4.0)),
        "tile_rows": draw_tile_rows(jax.random.fold_in(jax.random.fold_in(splits[6], part), 71), part),
        "params": scatter_about(part_splits[3], (D, F), 1.0, 5.0, ((0, 4),)),
        "first_moment": scatter_about(part_splits[4], (D, F), 0.1, 0.6, ((0, 4),), jnp.float32),
        "second_moment": jnp.clip(jnp.exp(math.log(0.05) - 2.3025851 * jax.random.uniform(part_splits[5], (D, F), jnp.float32) ** steps_of(part_splits[5], (D, F), ((0, 4),), -0.2, 0.2)), 0.005, 0.05),
    }


beta_one = 0.9
beta_two = 0.95
learn_rate = 0.05
weight_decay = 0.1
epsilon = 1e-08

def adamw(grad, params, first_moment, second_moment):
    first_new = beta_one * first_moment + (1.0 - beta_one) * grad
    second_new = beta_two * second_moment + (1.0 - beta_two) * grad * grad
    update = first_new / (1.0 - beta_one ** 3) / (jnp.sqrt(second_new / (1.0 - beta_two ** 3)) + epsilon)
    weights = params.astype(jnp.float32)
    new_params = (weights - learn_rate * (update + weight_decay * weights)).astype(jnp.bfloat16)
    return (new_params, first_new, second_new)

def reference(activations, cotangent, tile_rows, params, first_moment, second_moment):
    within = lax.broadcasted_iota(jnp.int32, (TOKENS // TILE, TILE), 1)
    live = (within < tile_rows[:, None]).reshape(TOKENS, 1)
    masked = jnp.where(live, cotangent, jnp.zeros_like(cotangent))
    blocks_x = activations.reshape(TOKENS // TOK_DEV, TOK_DEV, D)
    blocks_g = masked.reshape(TOKENS // TOK_DEV, TOK_DEV, F)

    def accumulate(total, pair):
        term = lax.dot_general(pair[0], pair[1], (((0,), (0,)), ((), ())), preferred_element_type=jnp.float32)
        return (total + term, None)
    grad, _ = lax.scan(accumulate, jnp.zeros((D, F), jnp.float32), (blocks_x, blocks_g))
    new_params, first_new, second_new = adamw(grad, params, first_moment, second_moment)
    return (new_params, first_new, second_new)
```

```python
import functools

import jax
import jax.numpy as jnp
from jax import lax
from jax.experimental import pallas as pl
from jax.experimental.pallas import tpu as pltpu
from jax.sharding import PartitionSpec as P

beta_one = 0.9
beta_two = 0.95
learn_rate = 0.05
weight_decay = 0.1
epsilon = 1e-08

MESH = pl.DeviceIdType.MESH
SIDE = 4
ROWS = 32
COLS = 768
HALF = 384
BLOCK = SIDE * SIDE * ROWS
LANES = 128
LEVELS = 32767.0
F32 = jnp.float32


def adamw(grad, params, first_moment, second_moment):
    first_new = beta_one * first_moment + (1.0 - beta_one) * grad
    second_new = beta_two * second_moment + (1.0 - beta_two) * grad * grad
    update = (
        first_new / (1.0 - beta_one**3) / (jnp.sqrt(second_new / (1.0 - beta_two**3)) + epsilon)
    )
    weights = params.astype(F32)
    new_params = (weights - learn_rate * (update + weight_decay * weights)).astype(jnp.bfloat16)
    return (new_params, first_new, second_new)


def spread(row, columns):
    return jnp.concatenate([row] * (columns // LANES), axis=1)


def encode(value, code_ref, scale_ref):
    columns = value.shape[1]
    top = jnp.max(jnp.abs(value), axis=0, keepdims=True)
    peak = top[:, :LANES]
    for at in range(LANES, columns, LANES):
        peak = jnp.maximum(peak, top[:, at : at + LANES])
    peak = jnp.maximum(peak, 1e-30)
    code = jnp.round(value * spread(LEVELS / peak, columns)).astype(jnp.int32)
    code_ref[...] = code.astype(jnp.int16).reshape(code_ref.shape)
    scale_ref[...] = jnp.broadcast_to(peak * (1.0 / LEVELS), scale_ref.shape)


def decode(code, scale_ref):
    columns = code.shape[-1]
    value = code.reshape(-1, columns).astype(jnp.int32).astype(F32)
    return value * spread(scale_ref[0:1, :], columns)


def kernel(
    acts, cot, tiles, params, first, second,
    out, first_out, second_out,
    act_buf, cot_buf, mask_buf, par_buf, mom_buf, acc, tmp,
    sib_code, sib_scale, one_code, one_scale, two_code, two_scale, z_code, z_scale,
    part, whole,
    load_sem, sib_sem, one_sem, two_sem, z_sem, far_sem, up_sem, over_sem, twin_sem,
):
    exp, inner, outer = lax.axis_index("exp"), lax.axis_index("inner"), lax.axis_index("outer")
    x, y = outer // SIDE, outer % SIDE
    plane, core = inner // 2, inner % 2
    other = 1 - plane

    twin = (exp, plane * 2 + 1 - core, outer)
    far = (exp, other * 2 + core, outer)

    def along(axis, step):
        if axis == 0:
            return (exp, inner, (x + step) % SIDE * SIDE + y)
        return (exp, inner, x * SIDE + (y + step) % SIDE)

    def column(block, who):
        return pl.multiple_of((block * 2 + who) * BLOCK, BLOCK)

    blocks = (other, plane)
    load_cot = pltpu.make_async_copy(cot, cot_buf, load_sem.at[0])
    load_cot.start()
    loads = []
    for b in range(2):
        for own in range(2):
            who = core if own else 1 - core
            load = pltpu.make_async_copy(
                acts.at[:, pl.ds(column(blocks[b], who), BLOCK)],
                act_buf.at[2 * b + own],
                load_sem.at[1 + 2 * b + own],
            )
            load.start()
            loads.append(load)
    mine = pl.ds(pl.multiple_of(outer * ROWS, ROWS), ROWS)
    state = [
        pltpu.make_async_copy(params.at[mine, :], par_buf, load_sem.at[5]),
        pltpu.make_async_copy(first.at[mine, :], mom_buf.at[0], load_sem.at[6]),
        pltpu.make_async_copy(second.at[mine, :], mom_buf.at[1], load_sem.at[7]),
    ]
    for load in state:
        load.start()

    barrier = pltpu.get_barrier_semaphore()
    partners = [twin, far] + [along(a, s) for a in range(2) for s in (1, 2, 3)]
    for partner in partners:
        pl.semaphore_signal(barrier, inc=1, device_id=partner, device_id_type=MESH)

    load_cot.wait()
    tile = cot_buf.shape[0] // tiles.shape[0]
    within = lax.broadcasted_iota(jnp.int32, (tile, COLS), 0)
    for t in range(tiles.shape[0]):
        rows = pl.ds(t * tile, tile)
        value = cot_buf[rows, :]
        mask_buf[rows, :] = jnp.where(within < tiles[t], value, jnp.zeros_like(value))

    started = []

    def send(src, dst, sems, device):
        copy = pltpu.make_async_remote_copy(
            src_ref=src, dst_ref=dst, send_sem=sems.at[0], recv_sem=sems.at[1],
            device_id=device, device_id_type=MESH,
        )
        copy.start()
        started.append(copy)
        return copy

    def send_coded(value, code, scale, sems, device):
        encode(value, code.at[0], scale.at[0])
        return (
            send(scale.at[0], scale.at[1], sems.at[1], device),
            send(code.at[0], code.at[1], sems.at[0], device),
        )

    def arrived(copies):
        for copy in copies:
            copy.wait_recv()

    def product(at):
        loads[at].wait()
        return lax.dot_general(
            act_buf[at], mask_buf[...], (((0,), (0,)), ((), ())), preferred_element_type=F32
        )

    def to_twin(b):
        tmp[...] = product(2 * b)
        if b == 0:
            pl.semaphore_wait(barrier, len(partners))
        return send_coded(tmp[...], sib_code.at[b], sib_scale.at[b], sib_sem.at[b], twin)

    def own(b):
        acc[b] = product(2 * b + 1).reshape(SIDE, SIDE, ROWS, COLS)

    def halves(b, axis, at):
        if axis == 0:
            return acc[b, at, :, :, :HALF].reshape(SIDE * ROWS, HALF)
        return acc[b, :, at, :, HALF:].reshape(SIDE * ROWS, HALF)

    def phase_one(b, copies):
        arrived(copies)

        def add(at, carry):
            got = sib_code[b, 1, at]
            acc[b, at] += decode(got, sib_scale.at[b, 1]).reshape(SIDE, ROWS, COLS)
            return carry

        lax.fori_loop(0, SIDE, add, 0)
        sent = []
        for step in (2, 1, 3):
            for axis in range(2):
                at = ((x, y)[axis] + step) % SIDE
                sent.append(
                    send_coded(
                        halves(b, axis, at), one_code.at[b, axis, step - 1],
                        one_scale.at[b, axis, step - 1], one_sem.at[b, axis, step - 1],
                        along(axis, step),
                    )
                )
        return sent

    def phase_two(b, copies):
        for axis in range(2):
            total = halves(b, axis, (x, y)[axis])
            for pair, step in zip(copies[axis::2], (2, 1, 3), strict=True):
                arrived(pair)
                total += decode(one_code[b, axis, step - 1, 1], one_scale.at[b, axis, step - 1, 1])
            part[b, axis] = total.reshape(SIDE, ROWS, HALF)
        sent = []
        for step in (2, 1, 3):
            for axis in range(2):
                at = ((y, x)[axis] + step) % SIDE
                sent.append(
                    send_coded(
                        part[b, axis, at], two_code.at[b, axis, step - 1],
                        two_scale.at[b, axis, step - 1], two_sem.at[b, axis, step - 1],
                        along(1 - axis, step),
                    )
                )
        return sent

    def plane_sum(b, copies):
        sides = []
        for axis in range(2):
            total = part[b, axis, (y, x)[axis]]
            for pair, step in zip(copies[axis::2], (2, 1, 3), strict=True):
                arrived(pair)
                total += decode(two_code[b, axis, step - 1, 1], two_scale.at[b, axis, step - 1, 1])
            sides.append(total)
        return jnp.concatenate(sides, axis=1)

    twin_0 = to_twin(0)
    own(0)
    twin_1 = to_twin(1)
    one_0 = phase_one(0, twin_0)
    own(1)
    one_1 = phase_one(1, twin_1)
    two_0 = phase_two(0, one_0)
    two_1 = phase_two(1, one_1)
    z_sum = send_coded(plane_sum(0, two_0), z_code, z_scale, z_sem, far)
    grad = plane_sum(1, two_1)
    for load in state:
        load.wait()
    arrived(z_sum)
    grad += decode(z_code[1], z_scale.at[1])
    piece, first_new, second_new = adamw(grad, par_buf[...], mom_buf[0], mom_buf[1])
    first_out[...] = first_new
    second_out[...] = second_new
    whole[inner, x, y] = piece

    def gather_one(block):
        at = block * 2 + core
        sent = []
        for step in (2, 1, 3):
            for axis in range(2):
                ref = whole.at[at, x, y, :, pl.ds(axis * HALF, HALF)]
                sent.append(send(ref, ref, up_sem.at[block, axis, step - 1], along(axis, step)))
        return sent

    def gather_two(block, copies):
        at = block * 2 + core
        sent, shared = [], []
        for axis in range(2):
            arrived(copies[axis::2])
            if axis == 0:
                ref = whole.at[at, :, y, :, pl.ds(0, HALF)]
            else:
                ref = whole.at[at, x, :, :, pl.ds(HALF, HALF)]
            for step in (2, 1, 3):
                sent.append(send(ref, ref, over_sem.at[block, axis, step - 1], along(1 - axis, step)))
            shared.append(send(ref, ref, twin_sem.at[block, axis, 3], twin))
        return sent, shared

    def gather_twin(block, copies):
        at = block * 2 + core
        shared = []
        for axis in range(2):
            for copy, step in zip(copies[3 * axis : 3 * axis + 3], (2, 1, 3), strict=True):
                copy.wait_recv()
                if axis == 0:
                    ref = whole.at[at, :, (y + SIDE - step) % SIDE, :, pl.ds(0, HALF)]
                else:
                    ref = whole.at[at, (x + SIDE - step) % SIDE, :, :, pl.ds(HALF, HALF)]
                shared.append(send(ref, ref, twin_sem.at[block, axis, step - 1], twin))
        return shared

    ref = whole.at[inner, x, y]
    far_piece = send(ref, ref, far_sem, far)
    up_0 = gather_one(plane)
    over_0, shared = gather_two(plane, up_0)
    arrived([far_piece])
    up_1 = gather_one(other)
    shared += gather_twin(plane, over_0)
    over_1, more = gather_two(other, up_1)
    shared += more
    shared += gather_twin(other, over_1)
    arrived(shared)
    store = pltpu.make_async_copy(whole, out, load_sem.at[8])
    store.start()
    for copy in started:
        copy.wait_send()
    store.wait()


def shards(activations, cotangent, tile_rows, params, first_moment, second_moment):
    rows, depth = activations.shape
    count = depth // BLOCK
    bf16, i16 = jnp.bfloat16, jnp.int16
    anywhere = pl.BlockSpec(memory_space=pl.ANY)
    vmem = pl.BlockSpec(memory_space=pltpu.VMEM)
    dma = pltpu.SemaphoreType.DMA
    whole, first_new, second_new = pl.pallas_call(
        kernel,
        out_shape=(
            jax.ShapeDtypeStruct((count, SIDE, SIDE, ROWS, COLS), bf16),
            jax.ShapeDtypeStruct((ROWS, COLS), F32),
            jax.ShapeDtypeStruct((ROWS, COLS), F32),
        ),
        in_specs=[
            anywhere, anywhere, pl.BlockSpec(memory_space=pltpu.SMEM), anywhere, anywhere, anywhere,
        ],
        out_specs=(anywhere, vmem, vmem),
        scratch_shapes=[
            pltpu.VMEM((4, rows, BLOCK), bf16),
            pltpu.VMEM((rows, COLS), bf16),
            pltpu.VMEM((rows, COLS), bf16),
            pltpu.VMEM((ROWS, COLS), bf16),
            pltpu.VMEM((2, ROWS, COLS), F32),
            pltpu.VMEM((2, SIDE, SIDE, ROWS, COLS), F32),
            pltpu.VMEM((BLOCK, COLS), F32),
            pltpu.VMEM((2, 2, SIDE, SIDE * ROWS, COLS), i16),
            pltpu.VMEM((2, 2, 8, LANES), F32),
            pltpu.VMEM((2, 2, 3, 2, SIDE * ROWS, HALF), i16),
            pltpu.VMEM((2, 2, 3, 2, 8, LANES), F32),
            pltpu.VMEM((2, 2, 3, 2, ROWS, HALF), i16),
            pltpu.VMEM((2, 2, 3, 2, 8, LANES), F32),
            pltpu.VMEM((2, ROWS, COLS), i16),
            pltpu.VMEM((2, 8, LANES), F32),
            pltpu.VMEM((2, 2, SIDE, ROWS, HALF), F32),
            pltpu.VMEM((count, SIDE, SIDE, ROWS, COLS), bf16),
            dma((9,)),
            dma((2, 2, 2)),
            dma((2, 2, 3, 2, 2)),
            dma((2, 2, 3, 2, 2)),
            dma((2, 2)),
            dma((2,)),
            dma((2, 2, 3, 2)),
            dma((2, 2, 3, 2)),
            dma((2, 2, 4, 2)),
        ],
        compiler_params=pltpu.CompilerParams(
            collective_id=0, has_side_effects=True, vmem_limit_bytes=56 * 2**20
        ),
    )(activations, cotangent, tile_rows, params, first_moment, second_moment)
    return whole.reshape(depth, COLS), first_new, second_new


def solution(mesh):
    in_specs = (
        P(("exp", "inner", "outer"), None),
        P(("exp", "inner", "outer"), None),
        P(("exp", "inner", "outer")),
        P(("exp", "inner"), None),
        P(("exp", "inner"), None),
        P(("exp", "inner"), None),
    )
    out_specs = (
        P("exp", None),
        P(("exp", "inner", "outer"), None),
        P(("exp", "inner", "outer"), None),
    )
    return jax.shard_map(shards, mesh=mesh, in_specs=in_specs, out_specs=out_specs, check_vma=False)
```

```python
import functools

import jax
import jax.numpy as jnp
from jax import lax
from jax.experimental import pallas as pl
from jax.experimental.pallas import tpu as pltpu
from jax.sharding import PartitionSpec as P

beta_one = 0.9
beta_two = 0.95
learn_rate = 0.05
weight_decay = 0.1
epsilon = 1e-08

MESH = pl.DeviceIdType.MESH
SIDE = 4
ROWS = 32
COLS = 768
HALF = 384
GROUP = SIDE * ROWS
BLOCK = SIDE * GROUP
LANES = 128
LEVELS = 32767.0
PIECES = 8
F32 = jnp.float32


def adamw(grad, params, first_moment, second_moment):
    first_new = beta_one * first_moment + (1.0 - beta_one) * grad
    second_new = beta_two * second_moment + (1.0 - beta_two) * grad * grad
    update = (
        first_new / (1.0 - beta_one**3) / (jnp.sqrt(second_new / (1.0 - beta_two**3)) + epsilon)
    )
    weights = params.astype(F32)
    new_params = (weights - learn_rate * (update + weight_decay * weights)).astype(jnp.bfloat16)
    return (new_params, first_new, second_new)


def spread(row, columns):
    return jnp.concatenate([row] * (columns // LANES), axis=1)


def encode(value, code_ref, scale_ref):
    columns = value.shape[1]
    top = jnp.max(jnp.abs(value), axis=0, keepdims=True)
    peak = top[:, :LANES]
    for at in range(LANES, columns, LANES):
        peak = jnp.maximum(peak, top[:, at : at + LANES])
    peak = jnp.maximum(peak, 1e-30)
    code = jnp.round(value * spread(LEVELS / peak, columns)).astype(jnp.int32)
    code_ref[...] = code.astype(jnp.int16).reshape(code_ref.shape)
    scale_ref[...] = jnp.broadcast_to(peak * (1.0 / LEVELS), scale_ref.shape)


def decode(code, scale_ref):
    columns = code.shape[-1]
    value = code.reshape(-1, columns).astype(jnp.int32).astype(F32)
    return value * spread(scale_ref[0:1, :], columns)


def kernel(
    acts, cot, tiles, params, first, second,
    whole, first_out, second_out,
    act_buf, cot_buf, tile_buf, par_buf, mom_buf, acc, twin_half, part,
    one_code, two_code, z_code, scales, size,
    load_sem, sent_sem, sib_sem, one_sem, two_sem, z_sem, far_sem, up_sem, over_sem, twin_sem,
):
    exp, inner, outer = lax.axis_index("exp"), lax.axis_index("inner"), lax.axis_index("outer")
    place = (outer // SIDE, outer % SIDE)
    x, y = place
    plane, core = inner // 2, inner % 2
    other = 1 - plane

    twin = (exp, plane * 2 + 1 - core, outer)
    far = (exp, other * 2 + core, outer)

    def along(axis, step):
        if axis == 0:
            return (exp, inner, (x + step) % SIDE * SIDE + y)
        return (exp, inner, x * SIDE + (y + step) % SIDE)

    barrier = pltpu.get_barrier_semaphore()
    partners = [twin, far] + [along(a, s) for a in range(2) for s in (1, 2, 3)]
    for partner in partners:
        pl.semaphore_signal(barrier, inc=1, device_id=partner, device_id_type=MESH)

    blocks = (other, plane)

    def load_chunk(b, own):
        who = core if own else 1 - core
        at = pl.multiple_of((blocks[b] * 2 + who) * BLOCK, BLOCK)
        return pltpu.make_async_copy(
            acts.at[:, pl.ds(at, BLOCK)], act_buf.at[2 * b + own], load_sem.at[1 + 2 * b + own]
        )

    load_tiles = pltpu.make_async_copy(tiles, tile_buf, load_sem.at[8])
    load_cot = pltpu.make_async_copy(cot, cot_buf, load_sem.at[0])
    loads = [load_chunk(b, own) for b in range(2) for own in range(2)]
    mine = pl.ds(pl.multiple_of(outer * ROWS, ROWS), ROWS)
    state = [
        pltpu.make_async_copy(params.at[mine, :], par_buf, load_sem.at[5]),
        pltpu.make_async_copy(first.at[mine, :], mom_buf.at[0], load_sem.at[6]),
        pltpu.make_async_copy(second.at[mine, :], mom_buf.at[1], load_sem.at[7]),
    ]
    for load in [load_tiles, load_cot] + loads + state:
        load.start()

    load_tiles.wait()
    load_cot.wait()
    tile = cot_buf.shape[0] // tile_buf.shape[0]
    within = lax.broadcasted_iota(jnp.int32, (tile, COLS), 0)
    for t in range(tile_buf.shape[0]):
        rows = pl.ds(t * tile, tile)
        value = cot_buf[rows, :]
        cot_buf[rows, :] = jnp.where(within < tile_buf[t], value, jnp.zeros_like(value))

    def send(src, dst, send_sem, recv_sem, device):
        pltpu.make_async_remote_copy(
            src_ref=src, dst_ref=dst, send_sem=send_sem, recv_sem=recv_sem,
            device_id=device, device_id_type=MESH,
        ).start()

    def take(ref, sem):
        pltpu.make_async_copy(ref, ref, sem).wait()

    def send_coded(value, code, at, slot, sems, device):
        encode(value, code.at[(0,) + at], scales.at[0, slot])
        send(scales.at[0, slot], scales.at[1, slot], sent_sem.at[0], sems[1], device)
        send(code.at[(0,) + at], code.at[(1,) + at], sems[0], sems[1], device)

    def got(code, at, slot):
        return decode(code[(1,) + at], scales.at[1, slot])

    def product(at, pair):
        columns = pl.ds(pair * 2 * GROUP, 2 * GROUP)
        return lax.dot_general(
            act_buf[at, :, columns], cot_buf[...], (((0,), (0,)), ((), ())),
            preferred_element_type=F32,
        ).reshape(2, SIDE, ROWS, COLS)

    def to_twin(b):
        loads[2 * b].wait()
        for pair in range(2):
            acc[0, b, 2 * pair : 2 * pair + 2] = product(2 * b, pair)
            if b == 0 and pair == 0:
                pl.semaphore_wait(barrier, len(partners))
            xs = pl.ds(2 * pair, 2)
            send(acc.at[0, b, xs], twin_half.at[b, xs], sent_sem.at[1], sib_sem.at[b], twin)

    def own(b):
        loads[2 * b + 1].wait()
        for pair in range(2):
            acc[1, b, 2 * pair : 2 * pair + 2] = product(2 * b + 1, pair)

    def slab(ref, half, at):
        value = ref[at, :, :, :HALF] if half == 0 else ref[:, at, :, HALF:]
        return value.reshape(GROUP, HALF)

    def chip_sum(b, half, at):
        return slab(acc.at[1, b], half, at) + slab(twin_half.at[b], half, at)

    steps = (2, 1, 3)

    def slot_of(phase, b, half, step):
        return phase * 12 + b * 6 + half * 3 + step - 1

    def first_sends(b):
        take(twin_half.at[b], sib_sem.at[b])
        for step in steps:
            for half in range(2):
                value = chip_sum(b, half, (place[half] + step) % SIDE)
                send_coded(
                    value, one_code, (b, half, step - 1), slot_of(0, b, half, step),
                    (sent_sem.at[2], one_sem.at[b, half]), along(half, step),
                )

    def second_sends(b):
        for half in range(2):
            take(size, one_sem.at[b, half])
            value = chip_sum(b, half, place[half])
            for step in steps:
                value += got(one_code, (b, half, step - 1), slot_of(0, b, half, step))
            part[b, half] = value.reshape(SIDE, ROWS, HALF)
            for step in steps:
                send_coded(
                    part[b, half, (place[1 - half] + step) % SIDE], two_code,
                    (b, half, step - 1), slot_of(1, b, half, step),
                    (sent_sem.at[3], two_sem.at[b, half]), along(1 - half, step),
                )

    def plane_sum(b, half):
        take(size.at[pl.ds(0, 336), :], two_sem.at[b, half])
        total = part[b, half, place[1 - half]]
        for step in steps:
            total += got(two_code, (b, half, step - 1), slot_of(1, b, half, step))
        return total

    def far_sums():
        for half in range(2):
            send_coded(
                plane_sum(0, half), z_code, (half,), 24 + half,
                (sent_sem.at[4], z_sem.at[half]), far,
            )

    def columns(half):
        return pl.ds(half * HALF, HALF)

    def region(block, half, at):
        block = whole.at[block * 2 + core]
        if half == 0:
            return block.at[at, :, :, columns(half)]
        return block.at[:, at, :, columns(half)]

    def up(block, half):
        ref = whole.at[block * 2 + core, x, y, :, columns(half)]
        for step in steps:
            send(ref, ref, sent_sem.at[6], up_sem.at[block, half], along(1 - half, step))

    def step_adam(half):
        grad = plane_sum(1, half)
        take(size.at[pl.ds(0, 112), :], z_sem.at[half])
        grad += got(z_code, (half,), 24 + half)
        at = slice(half * HALF, (half + 1) * HALF)
        piece, first_new, second_new = adamw(
            grad, par_buf[:, at], mom_buf[0, :, at], mom_buf[1, :, at]
        )
        whole[inner, x, y, :, at] = piece
        ref = whole.at[inner, x, y, :, columns(half)]
        send(ref, ref, sent_sem.at[5], far_sem.at[half], far)
        up(plane, half)
        first_out[:, at] = first_new
        second_out[:, at] = second_new

    def gathered(block, half):
        take(whole.at[0, 0, pl.ds(0, 3), :, columns(0)], up_sem.at[block, half])

    def over(block, half, step):
        ref = region(block, half, place[half])
        send(ref, ref, sent_sem.at[7], over_sem.at[block, half, step - 1], along(half, step))

    def share(block, half, step):
        if step:
            take(whole.at[0, 0, pl.ds(0, 2)], over_sem.at[block, half, step - 1])
        ref = region(block, half, (place[half] + SIDE - step) % SIDE)
        send(ref, ref, sent_sem.at[8], twin_sem.at[0], twin)

    for b in range(2):
        to_twin(b)
        own(b)
    first_sends(0)
    first_sends(1)
    second_sends(0)
    second_sends(1)
    far_sums()
    for load in state:
        load.wait()
    for half in range(2):
        step_adam(half)
    for half in range(2):
        gathered(plane, half)
        over(plane, half, 1)
        over(plane, half, 3)
    for half in range(2):
        take(whole.at[0, 0, 0, :, columns(0)], far_sem.at[half])
        up(other, half)
    for half in range(2):
        over(plane, half, 2)
        share(plane, half, 0)
    for half in range(2):
        gathered(other, half)
        for step in steps:
            over(other, half, step)
    for half in range(2):
        share(other, half, 0)
        share(plane, half, 1)
        share(plane, half, 3)
    for half in range(2):
        share(plane, half, 2)
    for half in range(2):
        share(other, half, 1)
        share(other, half, 3)
    for half in range(2):
        share(other, half, 2)

    take(scales.at[0], sent_sem.at[0])
    take(acc.at[0], sent_sem.at[1])
    take(one_code.at[0], sent_sem.at[2])
    take(two_code.at[0], sent_sem.at[3])
    take(z_code.at[0], sent_sem.at[4])
    take(whole.at[0, 0, 0], sent_sem.at[5])
    take(whole.at[0, pl.ds(0, 3), pl.ds(0, 2)], sent_sem.at[6])
    take(whole.at[pl.ds(0, 3), pl.ds(0, 2)], sent_sem.at[7])
    take(whole.at[pl.ds(0, 2)], sent_sem.at[8])
    take(whole.at[pl.ds(0, 2)], twin_sem.at[0])


def hand_on(whole, first, second, out, first_out, second_out, sems):
    step = whole.shape[0] // PIECES
    copies = [
        pltpu.make_async_copy(first, first_out, sems.at[PIECES]),
        pltpu.make_async_copy(second, second_out, sems.at[PIECES + 1]),
    ]
    for i in range(PIECES):
        rows = pl.ds(i * step, step)
        copies.append(pltpu.make_async_copy(whole.at[rows, :], out.at[rows, :], sems.at[i]))
    for copy in copies:
        copy.start()
    for copy in copies:
        copy.wait()


def shards(activations, cotangent, tile_rows, params, first_moment, second_moment):
    rows, depth = activations.shape
    count = depth // BLOCK
    bf16, i16 = jnp.bfloat16, jnp.int16
    anywhere = pl.BlockSpec(memory_space=pltpu.HBM)
    vmem = pl.BlockSpec(memory_space=pltpu.VMEM)
    dma = pltpu.SemaphoreType.DMA
    whole, first_new, second_new = pl.pallas_call(
        kernel,
        out_shape=(
            pltpu.VMEM((count, SIDE, SIDE, ROWS, COLS), bf16),
            pltpu.VMEM((ROWS, COLS), F32),
            pltpu.VMEM((ROWS, COLS), F32),
        ),
        in_specs=[
            anywhere, anywhere, anywhere, anywhere, anywhere, anywhere,
        ],
        out_specs=(vmem, vmem, vmem),
        scratch_shapes=[
            pltpu.VMEM((4, rows, BLOCK), bf16),
            pltpu.VMEM((rows, COLS), bf16),
            pltpu.SMEM(tile_rows.shape, jnp.int32),
            pltpu.VMEM((ROWS, COLS), bf16),
            pltpu.VMEM((2, ROWS, COLS), F32),
            pltpu.VMEM((2, 2, SIDE, SIDE, ROWS, COLS), F32),
            pltpu.VMEM((2, SIDE, SIDE, ROWS, COLS), F32),
            pltpu.VMEM((2, 2, SIDE, ROWS, HALF), F32),
            pltpu.VMEM((2, 2, 2, 3, GROUP, HALF), i16),
            pltpu.VMEM((2, 2, 2, 3, ROWS, HALF), i16),
            pltpu.VMEM((2, 2, ROWS, HALF), i16),
            pltpu.VMEM((2, 26, 8, LANES), F32),
            pltpu.VMEM((1200, LANES), i16),
            dma((9,)),
            dma((9,)),
            dma((2,)),
            dma((2, 2)),
            dma((2, 2)),
            dma((2,)),
            dma((2,)),
            dma((2, 2)),
            dma((2, 2, 3)),
            dma((1,)),
        ],
        compiler_params=pltpu.CompilerParams(
            collective_id=0, has_side_effects=True, vmem_limit_bytes=58 * 2**20
        ),
    )(activations, cotangent, tile_rows, params, first_moment, second_moment)
    whole = whole.reshape(depth, COLS)
    return pl.pallas_call(
        hand_on,
        out_shape=tuple(jax.ShapeDtypeStruct(a.shape, a.dtype) for a in (whole, first_new, second_new)),
        in_specs=[pl.BlockSpec(memory_space=pl.ANY)] * 3,
        out_specs=(anywhere,) * 3,
        scratch_shapes=[dma((PIECES + 2,))],
        compiler_params=pltpu.CompilerParams(vmem_limit_bytes=4 * 2**20),
    )(whole, first_new, second_new)


def solution(mesh):
    in_specs = (
        P(("exp", "inner", "outer"), None),
        P(("exp", "inner", "outer"), None),
        P(("exp", "inner", "outer")),
        P(("exp", "inner"), None),
        P(("exp", "inner"), None),
        P(("exp", "inner"), None),
    )
    out_specs = (
        P("exp", None),
        P(("exp", "inner", "outer"), None),
        P(("exp", "inner", "outer"), None),
    )
    return jax.shard_map(shards, mesh=mesh, in_specs=in_specs, out_specs=out_specs, check_vma=False)
```

```python
import functools

import jax
import jax.numpy as jnp
from jax import lax
from jax.experimental import pallas as pl
from jax.experimental.pallas import tpu as pltpu
from jax.sharding import PartitionSpec as P

beta_one = 0.9
beta_two = 0.95
learn_rate = 0.05
weight_decay = 0.1
epsilon = 1e-08

MESH = pl.DeviceIdType.MESH
SIDE = 4
ROWS = 32
COLS = 768
HALF = 384
GROUP = SIDE * ROWS
BLOCK = SIDE * GROUP
LANES = 128
LEVELS = 32767.0
PIECES = 16
F32 = jnp.float32


def adamw(grad, params, first_moment, second_moment):
    first_new = beta_one * first_moment + (1.0 - beta_one) * grad
    second_new = beta_two * second_moment + (1.0 - beta_two) * grad * grad
    update = (
        first_new / (1.0 - beta_one**3) / (jnp.sqrt(second_new / (1.0 - beta_two**3)) + epsilon)
    )
    weights = params.astype(F32)
    new_params = (weights - learn_rate * (update + weight_decay * weights)).astype(jnp.bfloat16)
    return (new_params, first_new, second_new)


def spread(row, columns):
    return jnp.concatenate([row] * (columns // LANES), axis=1)


def encode(value, code_ref, scale_ref):
    columns = value.shape[1]
    top = jnp.max(jnp.abs(value), axis=0, keepdims=True)
    peak = top[:, :LANES]
    for at in range(LANES, columns, LANES):
        peak = jnp.maximum(peak, top[:, at : at + LANES])
    peak = jnp.maximum(peak, 1e-30)
    code = jnp.round(value * spread(LEVELS / peak, columns)).astype(jnp.int32)
    code_ref[...] = code.astype(jnp.int16).reshape(code_ref.shape)
    scale_ref[...] = jnp.broadcast_to(peak * (1.0 / LEVELS), scale_ref.shape)


def decode(code, scale_ref):
    columns = code.shape[-1]
    value = code.reshape(-1, columns).astype(jnp.int32).astype(F32)
    return value * spread(scale_ref[0:1, :], columns)


def kernel(
    acts, cot, tiles, params, first, second,
    whole, first_out, second_out,
    act_buf, cot_buf, tile_buf, par_buf, mom_buf, acc, twin_half, part,
    one_code, two_code, z_code, scales, size,
    load_sem, sent_sem, sib_sem, one_sem, two_sem, z_sem, far_sem, up_sem, over_sem, twin_sem,
):
    exp, inner, outer = lax.axis_index("exp"), lax.axis_index("inner"), lax.axis_index("outer")
    place = (outer // SIDE, outer % SIDE)
    x, y = place
    plane, core = inner // 2, inner % 2
    other = 1 - plane

    twin = (exp, plane * 2 + 1 - core, outer)
    far = (exp, other * 2 + core, outer)

    def along(axis, step):
        if axis == 0:
            return (exp, inner, (x + step) % SIDE * SIDE + y)
        return (exp, inner, x * SIDE + (y + step) % SIDE)

    barrier = pltpu.get_barrier_semaphore()
    partners = [twin, far] + [along(a, s) for a in range(2) for s in (1, 2, 3)]
    for partner in partners:
        pl.semaphore_signal(barrier, inc=1, device_id=partner, device_id_type=MESH)

    blocks = (other, plane)

    def load_chunk(b, own):
        who = core if own else 1 - core
        at = pl.multiple_of((blocks[b] * 2 + who) * BLOCK, BLOCK)
        return pltpu.make_async_copy(
            acts.at[:, pl.ds(at, BLOCK)], act_buf.at[2 * b + own], load_sem.at[1 + 2 * b + own]
        )

    load_tiles = pltpu.make_async_copy(tiles, tile_buf, load_sem.at[8])
    load_cot = pltpu.make_async_copy(cot, cot_buf, load_sem.at[0])
    loads = [load_chunk(b, own) for b in range(2) for own in range(2)]
    mine = pl.ds(pl.multiple_of(outer * ROWS, ROWS), ROWS)
    state = [
        pltpu.make_async_copy(params.at[mine, :], par_buf, load_sem.at[5]),
        pltpu.make_async_copy(first.at[mine, :], mom_buf.at[0], load_sem.at[6]),
        pltpu.make_async_copy(second.at[mine, :], mom_buf.at[1], load_sem.at[7]),
    ]
    for load in [load_tiles, load_cot, loads[0]]:
        load.start()

    load_tiles.wait()
    load_cot.wait()
    for load in loads[1:] + state:
        load.start()
    tile = cot_buf.shape[0] // tile_buf.shape[0]
    within = lax.broadcasted_iota(jnp.int32, (tile, COLS), 0)
    for t in range(tile_buf.shape[0]):
        rows = pl.ds(t * tile, tile)
        value = cot_buf[rows, :]
        cot_buf[rows, :] = jnp.where(within < tile_buf[t], value, jnp.zeros_like(value))

    def send(src, dst, send_sem, recv_sem, device):
        pltpu.make_async_remote_copy(
            src_ref=src, dst_ref=dst, send_sem=send_sem, recv_sem=recv_sem,
            device_id=device, device_id_type=MESH,
        ).start()

    def take(ref, sem):
        pltpu.make_async_copy(ref, ref, sem).wait()

    def send_coded(value, code, at, slot, sems, device):
        encode(value, code.at[(0,) + at], scales.at[0, slot])
        send(scales.at[0, slot], scales.at[1, slot], sent_sem.at[0], sems[1], device)
        send(code.at[(0,) + at], code.at[(1,) + at], sems[0], sems[1], device)

    def got(code, at, slot):
        return decode(code[(1,) + at], scales.at[1, slot])

    def product(at, pair):
        columns = pl.ds(pair * 2 * GROUP, 2 * GROUP)
        return lax.dot_general(
            act_buf[at, :, columns], cot_buf[...], (((0,), (0,)), ((), ())),
            preferred_element_type=F32,
        ).reshape(2, SIDE, ROWS, COLS)

    def to_twin(b, pair):
        xs = pl.ds(2 * pair, 2)
        send(acc.at[0, b, xs], twin_half.at[b, xs], sent_sem.at[1], sib_sem.at[b], twin)

    def others(b):
        loads[2 * b].wait()
        for pair in range(2):
            acc[0, b, 2 * pair : 2 * pair + 2] = product(2 * b, pair)
            if b == 0:
                if pair == 0:
                    pl.semaphore_wait(barrier, len(partners))
                to_twin(b, pair)

    def own(b):
        loads[2 * b + 1].wait()
        for pair in range(2):
            acc[1, b, 2 * pair : 2 * pair + 2] = product(2 * b + 1, pair)

    def slab(ref, half, at):
        value = ref[at, :, :, :HALF] if half == 0 else ref[:, at, :, HALF:]
        return value.reshape(GROUP, HALF)

    def chip_sum(b, half, at):
        return slab(acc.at[1, b], half, at) + slab(twin_half.at[b], half, at)

    steps = (1, 3, 2)

    def slot_of(phase, b, half, step):
        return phase * 12 + b * 6 + half * 3 + step - 1

    def first_sends(b):
        for step in steps:
            for half in range(2):
                value = chip_sum(b, half, (place[half] + step) % SIDE)
                send_coded(
                    value, one_code, (b, half, step - 1), slot_of(0, b, half, step),
                    (sent_sem.at[2], one_sem.at[b, half]), along(half, step),
                )

    def second_sends(b):
        for half in range(2):
            take(size, one_sem.at[b, half])
            value = chip_sum(b, half, place[half])
            for step in steps:
                value += got(one_code, (b, half, step - 1), slot_of(0, b, half, step))
            part[b, half] = value.reshape(SIDE, ROWS, HALF)
            for step in steps:
                send_coded(
                    part[b, half, (place[1 - half] + step) % SIDE], two_code,
                    (b, half, step - 1), slot_of(1, b, half, step),
                    (sent_sem.at[3], two_sem.at[b, half]), along(1 - half, step),
                )

    def plane_sum(b, half):
        take(size.at[pl.ds(0, 336), :], two_sem.at[b, half])
        total = part[b, half, place[1 - half]]
        for step in steps:
            total += got(two_code, (b, half, step - 1), slot_of(1, b, half, step))
        return total

    def far_sums():
        for half in range(2):
            send_coded(
                plane_sum(0, half), z_code, (half,), 24 + half,
                (sent_sem.at[4], z_sem.at[half]), far,
            )

    def columns(half):
        return pl.ds(half * HALF, HALF)

    def region(block, half, at):
        block = whole.at[block * 2 + core]
        if half == 0:
            return block.at[at, :, :, columns(half)]
        return block.at[:, at, :, columns(half)]

    def up(block, half):
        ref = whole.at[block * 2 + core, x, y, :, columns(half)]
        for step in steps:
            send(ref, ref, sent_sem.at[6], up_sem.at[block, half, step - 1], along(1 - half, step))

    def over(block, half, piece, some=steps):
        if piece:
            take(whole.at[0, 0, 0, :, columns(0)], up_sem.at[block, half, piece - 1])
        at = (place[1 - half] + SIDE - piece) % SIDE
        row, col = (x, at) if half == 0 else (at, y)
        ref = whole.at[block * 2 + core, row, col, :, columns(half)]
        for step in some:
            send(ref, ref, sent_sem.at[7], over_sem.at[block, half, step - 1], along(half, step))

    def step_adam(half):
        grad = plane_sum(1, half)
        take(size.at[pl.ds(0, 112), :], z_sem.at[half])
        grad += got(z_code, (half,), 24 + half)
        at = slice(half * HALF, (half + 1) * HALF)
        piece, first_new, second_new = adamw(
            grad, par_buf[:, at], mom_buf[0, :, at], mom_buf[1, :, at]
        )
        whole[inner, x, y, :, at] = piece
        ref = whole.at[inner, x, y, :, columns(half)]
        send(ref, ref, sent_sem.at[5], far_sem.at[half], far)
        up(plane, half)
        first_out[:, at] = first_new
        second_out[:, at] = second_new

    def relay(half):
        for way, step in enumerate((1, 3)):
            take(whole.at[0, 0, pl.ds(0, 2)], over_sem.at[plane, half, step - 1])
            at, some = (place[half] + SIDE - step) % SIDE, pl.ds(2 * way, 2)
            block = whole.at[inner]
            if half == 0:
                ref = block.at[at, some, :, columns(half)]
            else:
                ref = block.at[some, at, :, columns(half)]
            send(ref, ref, sent_sem.at[7], over_sem.at[plane, half, 1], along(half, step))

    def share(block, half, step, here=False):
        if step and not here:
            take(whole.at[0, 0, pl.ds(0, 2)], over_sem.at[block, half, step - 1])
        ref = region(block, half, (place[half] + SIDE - step) % SIDE)
        send(ref, ref, sent_sem.at[8], twin_sem.at[0], twin)

    for b in range(2):
        others(b)
        own(b)
    take(twin_half.at[0], sib_sem.at[0])
    to_twin(1, 0)
    to_twin(1, 1)
    first_sends(0)
    take(twin_half.at[1], sib_sem.at[1])
    first_sends(1)
    second_sends(0)
    far_sums()
    second_sends(1)
    for load in state:
        load.wait()
    for half in range(2):
        step_adam(half)
    for half in range(2):
        over(plane, half, 0, (1, 3))
    for piece in (1, 3, 2):
        for half in range(2):
            over(plane, half, piece, (1, 3))
    for half in range(2):
        take(whole.at[0, 0, 0, :, columns(0)], far_sem.at[half])
        up(other, half)
        over(other, half, 0)
    for half in range(2):
        relay(half)
    for half in range(2):
        share(plane, half, 0)
    for piece in (1, 3, 2):
        for half in range(2):
            over(other, half, piece)
    for half in range(2):
        share(other, half, 0)
        share(plane, half, 1, True)
        share(plane, half, 3, True)
    for half in range(2):
        share(plane, half, 2)
    for half in range(2):
        share(other, half, 1)
        share(other, half, 3)
    for half in range(2):
        share(other, half, 2)

    take(scales.at[0], sent_sem.at[0])
    take(acc.at[0], sent_sem.at[1])
    take(one_code.at[0], sent_sem.at[2])
    take(two_code.at[0], sent_sem.at[3])
    take(z_code.at[0], sent_sem.at[4])
    take(whole.at[0, 0, 0], sent_sem.at[5])
    take(whole.at[0, pl.ds(0, 3), pl.ds(0, 2)], sent_sem.at[6])
    take(whole.at[pl.ds(0, 3), pl.ds(0, 2)], sent_sem.at[7])
    take(whole.at[pl.ds(0, 2)], sent_sem.at[8])
    take(whole.at[pl.ds(0, 2)], twin_sem.at[0])


def hand_on(whole, first, second, out, first_out, second_out, sems):
    step = whole.shape[0] // PIECES
    copies = [
        pltpu.make_async_copy(first, first_out, sems.at[PIECES]),
        pltpu.make_async_copy(second, second_out, sems.at[PIECES + 1]),
    ]
    for i in range(PIECES):
        rows = pl.ds(i * step, step)
        copies.append(pltpu.make_async_copy(whole.at[rows, :], out.at[rows, :], sems.at[i]))
    for copy in copies:
        copy.start()
    for copy in copies:
        copy.wait()


def shards(activations, cotangent, tile_rows, params, first_moment, second_moment):
    rows, depth = activations.shape
    count = depth // BLOCK
    bf16, i16 = jnp.bfloat16, jnp.int16
    anywhere = pl.BlockSpec(memory_space=pltpu.HBM)
    vmem = pl.BlockSpec(memory_space=pltpu.VMEM)
    dma = pltpu.SemaphoreType.DMA
    whole, first_new, second_new = pl.pallas_call(
        kernel,
        out_shape=(
            pltpu.VMEM((count, SIDE, SIDE, ROWS, COLS), bf16),
            pltpu.VMEM((ROWS, COLS), F32),
            pltpu.VMEM((ROWS, COLS), F32),
        ),
        in_specs=[
            anywhere, anywhere, anywhere, anywhere, anywhere, anywhere,
        ],
        out_specs=(vmem, vmem, vmem),
        scratch_shapes=[
            pltpu.VMEM((4, rows, BLOCK), bf16),
            pltpu.VMEM((rows, COLS), bf16),
            pltpu.SMEM(tile_rows.shape, jnp.int32),
            pltpu.VMEM((ROWS, COLS), bf16),
            pltpu.VMEM((2, ROWS, COLS), F32),
            pltpu.VMEM((2, 2, SIDE, SIDE, ROWS, COLS), F32),
            pltpu.VMEM((2, SIDE, SIDE, ROWS, COLS), F32),
            pltpu.VMEM((2, 2, SIDE, ROWS, HALF), F32),
            pltpu.VMEM((2, 2, 2, 3, GROUP, HALF), i16),
            pltpu.VMEM((2, 2, 2, 3, ROWS, HALF), i16),
            pltpu.VMEM((2, 2, ROWS, HALF), i16),
            pltpu.VMEM((2, 26, 8, LANES), F32),
            pltpu.VMEM((1200, LANES), i16),
            dma((9,)),
            dma((9,)),
            dma((2,)),
            dma((2, 2)),
            dma((2, 2)),
            dma((2,)),
            dma((2,)),
            dma((2, 2, 3)),
            dma((2, 2, 3)),
            dma((1,)),
        ],
        compiler_params=pltpu.CompilerParams(
            collective_id=0, has_side_effects=True, vmem_limit_bytes=58 * 2**20
        ),
    )(activations, cotangent, tile_rows, params, first_moment, second_moment)
    whole = whole.reshape(depth, COLS)
    return pl.pallas_call(
        hand_on,
        out_shape=tuple(jax.ShapeDtypeStruct(a.shape, a.dtype) for a in (whole, first_new, second_new)),
        in_specs=[pl.BlockSpec(memory_space=pl.ANY)] * 3,
        out_specs=(anywhere,) * 3,
        scratch_shapes=[dma((PIECES + 2,))],
        compiler_params=pltpu.CompilerParams(vmem_limit_bytes=4 * 2**20),
    )(whole, first_new, second_new)


def solution(mesh):
    in_specs = (
        P(("exp", "inner", "outer"), None),
        P(("exp", "inner", "outer"), None),
        P(("exp", "inner", "outer")),
        P(("exp", "inner"), None),
        P(("exp", "inner"), None),
        P(("exp", "inner"), None),
    )
    out_specs = (
        P("exp", None),
        P(("exp", "inner", "outer"), None),
        P(("exp", "inner", "outer"), None),
    )
    return jax.shard_map(shards, mesh=mesh, in_specs=in_specs, out_specs=out_specs, check_vma=False)
```

```python
import functools

import jax
import jax.numpy as jnp
from jax import lax
from jax.experimental import pallas as pl
from jax.experimental.pallas import tpu as pltpu
from jax.sharding import PartitionSpec as P

beta_one = 0.9
beta_two = 0.95
learn_rate = 0.05
weight_decay = 0.1
epsilon = 1e-08

MESH = pl.DeviceIdType.MESH
SIDE = 4
ROWS = 32
COLS = 768
HALF = 384
GROUP = SIDE * ROWS
BLOCK = SIDE * GROUP
LANES = 128
LEVELS = 32767.0
PIECES = 16
F32 = jnp.float32


def adamw(grad, params, first_moment, second_moment):
    first_new = beta_one * first_moment + (1.0 - beta_one) * grad
    second_new = beta_two * second_moment + (1.0 - beta_two) * grad * grad
    update = (
        first_new / (1.0 - beta_one**3) / (jnp.sqrt(second_new / (1.0 - beta_two**3)) + epsilon)
    )
    weights = params.astype(F32)
    new_params = (weights - learn_rate * (update + weight_decay * weights)).astype(jnp.bfloat16)
    return (new_params, first_new, second_new)


def spread(row, columns):
    return jnp.concatenate([row] * (columns // LANES), axis=1)


def encode(value, code_ref, scale_ref):
    columns = value.shape[1]
    top = jnp.max(jnp.abs(value), axis=0, keepdims=True)
    peak = top[:, :LANES]
    for at in range(LANES, columns, LANES):
        peak = jnp.maximum(peak, top[:, at : at + LANES])
    peak = jnp.maximum(peak, 1e-30)
    code = jnp.round(value * spread(LEVELS / peak, columns)).astype(jnp.int32)
    code_ref[...] = code.astype(jnp.int16).reshape(code_ref.shape)
    scale_ref[...] = jnp.broadcast_to(peak * (1.0 / LEVELS), scale_ref.shape)


def decode(code, scale_ref):
    columns = code.shape[-1]
    value = code.reshape(-1, columns).astype(jnp.int32).astype(F32)
    return value * spread(scale_ref[0:1, :], columns)


def kernel(
    acts, cot, tiles, params, first, second,
    whole, first_out, second_out,
    act_buf, cot_buf, tile_buf, par_buf, mom_buf, acc, twin_half, part,
    one_code, two_code, z_code, scales, size,
    load_sem, sent_sem, sib_sem, one_sem, two_sem, z_sem, far_sem, up_sem, over_sem, twin_sem,
):
    exp, inner, outer = lax.axis_index("exp"), lax.axis_index("inner"), lax.axis_index("outer")
    place = (outer // SIDE, outer % SIDE)
    x, y = place
    plane, core = inner // 2, inner % 2
    other = 1 - plane

    twin = (exp, plane * 2 + 1 - core, outer)
    far = (exp, other * 2 + core, outer)

    def along(axis, step):
        if axis == 0:
            return (exp, inner, (x + step) % SIDE * SIDE + y)
        return (exp, inner, x * SIDE + (y + step) % SIDE)

    barrier = pltpu.get_barrier_semaphore()
    partners = [twin, far] + [along(a, s) for a in range(2) for s in (1, 2, 3)]
    for partner in partners:
        pl.semaphore_signal(barrier, inc=1, device_id=partner, device_id_type=MESH)

    blocks = (other, plane)

    def load_chunk(b, own):
        who = core if own else 1 - core
        at = pl.multiple_of((blocks[b] * 2 + who) * BLOCK, BLOCK)
        return pltpu.make_async_copy(
            acts.at[:, pl.ds(at, BLOCK)], act_buf.at[2 * b + own], load_sem.at[1 + 2 * b + own]
        )

    load_tiles = pltpu.make_async_copy(tiles, tile_buf, load_sem.at[8])
    load_cot = pltpu.make_async_copy(cot, cot_buf, load_sem.at[0])
    loads = [load_chunk(b, own) for b in range(2) for own in range(2)]
    mine = pl.ds(pl.multiple_of(outer * ROWS, ROWS), ROWS)
    state = [
        pltpu.make_async_copy(params.at[mine, :], par_buf, load_sem.at[5]),
        pltpu.make_async_copy(first.at[mine, :], mom_buf.at[0], load_sem.at[6]),
        pltpu.make_async_copy(second.at[mine, :], mom_buf.at[1], load_sem.at[7]),
    ]
    for load in [load_tiles, load_cot, loads[0]]:
        load.start()

    load_tiles.wait()
    load_cot.wait()
    for load in loads[1:] + state:
        load.start()
    tile = cot_buf.shape[0] // tile_buf.shape[0]
    within = lax.broadcasted_iota(jnp.int32, (tile, COLS), 0)
    for t in range(tile_buf.shape[0]):
        rows = pl.ds(t * tile, tile)
        value = cot_buf[rows, :]
        cot_buf[rows, :] = jnp.where(within < tile_buf[t], value, jnp.zeros_like(value))

    def send(src, dst, send_sem, recv_sem, device):
        pltpu.make_async_remote_copy(
            src_ref=src, dst_ref=dst, send_sem=send_sem, recv_sem=recv_sem,
            device_id=device, device_id_type=MESH,
        ).start()

    def take(ref, sem):
        pltpu.make_async_copy(ref, ref, sem).wait()

    def send_coded(value, code, at, slot, sems, device):
        encode(value, code.at[(0,) + at], scales.at[0, slot])
        send(scales.at[0, slot], scales.at[1, slot], sent_sem.at[0], sems[1], device)
        send(code.at[(0,) + at], code.at[(1,) + at], sems[0], sems[1], device)

    def got(code, at, slot):
        return decode(code[(1,) + at], scales.at[1, slot])

    def product(at, pair):
        columns = pl.ds(pair * 2 * GROUP, 2 * GROUP)
        return lax.dot_general(
            act_buf[at, :, columns], cot_buf[...], (((0,), (0,)), ((), ())),
            preferred_element_type=F32,
        ).reshape(2, SIDE, ROWS, COLS)

    def to_twin(b, pair):
        xs = pl.ds(2 * pair, 2)
        send(acc.at[0, b, xs], twin_half.at[b, xs], sent_sem.at[1], sib_sem.at[b], twin)

    def others(b):
        loads[2 * b].wait()
        for pair in range(2):
            acc[0, b, 2 * pair : 2 * pair + 2] = product(2 * b, pair)
            if b == 0:
                if pair == 0:
                    pl.semaphore_wait(barrier, len(partners))
                to_twin(b, pair)

    def own(b):
        loads[2 * b + 1].wait()
        for pair in range(2):
            acc[1, b, 2 * pair : 2 * pair + 2] = product(2 * b + 1, pair)

    def slab(ref, half, at):
        value = ref[at, :, :, :HALF] if half == 0 else ref[:, at, :, HALF:]
        return value.reshape(GROUP, HALF)

    def chip_sum(b, half, at):
        return slab(acc.at[1, b], half, at) + slab(twin_half.at[b], half, at)

    steps = (1, 3, 2)

    def slot_of(phase, b, half, step):
        return phase * 12 + b * 6 + half * 3 + step - 1

    def first_sends(b):
        for step in steps:
            for half in range(2):
                value = chip_sum(b, half, (place[half] + step) % SIDE)
                send_coded(
                    value, one_code, (b, half, step - 1), slot_of(0, b, half, step),
                    (sent_sem.at[2], one_sem.at[b, half]), along(half, step),
                )

    def chip_piece(b, half, second):
        row, col = (x, second) if half == 0 else (second, y)
        cols = slice(half * HALF, (half + 1) * HALF)
        value = acc[1, b, row, col, :, cols] + twin_half[b, row, col, :, cols]
        for step in steps:
            value += got(one_code, (b, half, step - 1, second), slot_of(0, b, half, step))
        return value

    def second_sends(b):
        for half in range(2):
            take(size, one_sem.at[b, half])
            for step in steps:
                send_coded(
                    chip_piece(b, half, (place[1 - half] + step) % SIDE), two_code,
                    (b, half, step - 1), slot_of(1, b, half, step),
                    (sent_sem.at[3], two_sem.at[b, half]), along(1 - half, step),
                )
        for half in range(2):
            part[b, half] = chip_piece(b, half, place[1 - half])

    def plane_sum(b, half):
        take(size.at[pl.ds(0, 336), :], two_sem.at[b, half])
        total = part[b, half]
        for step in steps:
            total += got(two_code, (b, half, step - 1), slot_of(1, b, half, step))
        return total

    def far_sums():
        for half in range(2):
            send_coded(
                plane_sum(0, half), z_code, (half,), 24 + half,
                (sent_sem.at[4], z_sem.at[half]), far,
            )

    def columns(half):
        return pl.ds(half * HALF, HALF)

    def region(block, half, at):
        block = whole.at[block * 2 + core]
        if half == 0:
            return block.at[at, :, :, columns(half)]
        return block.at[:, at, :, columns(half)]

    def up(block, half):
        ref = whole.at[block * 2 + core, x, y, :, columns(half)]
        for step in steps:
            send(ref, ref, sent_sem.at[6], up_sem.at[block, half, step - 1], along(1 - half, step))

    def over(block, half, piece, some=steps):
        if piece:
            take(whole.at[0, 0, 0, :, columns(0)], up_sem.at[block, half, piece - 1])
        at = (place[1 - half] + SIDE - piece) % SIDE
        row, col = (x, at) if half == 0 else (at, y)
        ref = whole.at[block * 2 + core, row, col, :, columns(half)]
        for step in some:
            sem = over_sem.at[block, half, step - 1, 0 if piece < 2 else 1]
            send(ref, ref, sent_sem.at[7], sem, along(half, step))

    def step_adam(half):
        grad = plane_sum(1, half)
        take(size.at[pl.ds(0, 112), :], z_sem.at[half])
        grad += got(z_code, (half,), 24 + half)
        at = slice(half * HALF, (half + 1) * HALF)
        piece, first_new, second_new = adamw(
            grad, par_buf[:, at], mom_buf[0, :, at], mom_buf[1, :, at]
        )
        whole[inner, x, y, :, at] = piece
        ref = whole.at[inner, x, y, :, columns(half)]
        send(ref, ref, sent_sem.at[5], far_sem.at[half], far)
        up(plane, half)
        first_out[:, at] = first_new
        second_out[:, at] = second_new

    def landed(block, half, step, group):
        take(whole.at[0, 0, 0], over_sem.at[block, half, step - 1, group])

    def share_group(half, step, group):
        landed(other, half, step, group)
        at = (place[half] + SIDE - step) % SIDE
        for piece in ((0, 1), (3, 2))[group]:
            second = (place[1 - half] + SIDE - piece) % SIDE
            row, col = (at, second) if half == 0 else (second, at)
            ref = whole.at[other * 2 + core, row, col, :, columns(half)]
            send(ref, ref, sent_sem.at[8], twin_sem.at[0], twin)

    def relay(half):
        for way, step in enumerate((1, 3)):
            landed(plane, half, step, 0)
            landed(plane, half, step, 1)
            at, some = (place[half] + SIDE - step) % SIDE, pl.ds(2 * way, 2)
            block = whole.at[inner]
            if half == 0:
                ref = block.at[at, some, :, columns(half)]
            else:
                ref = block.at[some, at, :, columns(half)]
            send(ref, ref, sent_sem.at[7], over_sem.at[plane, half, 1, way], along(half, step))

    def share(block, half, step, here=False):
        if step and not here:
            landed(block, half, step, 0)
            landed(block, half, step, 1)
        ref = region(block, half, (place[half] + SIDE - step) % SIDE)
        send(ref, ref, sent_sem.at[8], twin_sem.at[0], twin)

    for b in range(2):
        others(b)
        own(b)
    take(twin_half.at[0], sib_sem.at[0])
    to_twin(1, 0)
    to_twin(1, 1)
    first_sends(0)
    take(twin_half.at[1], sib_sem.at[1])
    first_sends(1)
    second_sends(0)
    far_sums()
    second_sends(1)
    for load in state:
        load.wait()
    for half in range(2):
        step_adam(half)
    for half in range(2):
        over(plane, half, 0, (1, 3))
    for piece in (1, 3, 2):
        for half in range(2):
            over(plane, half, piece, (1, 3))
    for half in range(2):
        take(whole.at[0, 0, 0, :, columns(0)], far_sem.at[half])
        up(other, half)
        over(other, half, 0)
    for half in range(2):
        relay(half)
        share(plane, half, 1, True)
        share(plane, half, 3, True)
    for half in range(2):
        share(plane, half, 0)
    for piece in (1, 3, 2):
        for half in range(2):
            over(other, half, piece)
    for half in range(2):
        share(other, half, 0)
    for half in range(2):
        share(plane, half, 2)
    for group in range(2):
        for step in steps:
            for half in range(2):
                share_group(half, step, group)

    take(scales.at[0], sent_sem.at[0])
    take(acc.at[0], sent_sem.at[1])
    take(one_code.at[0], sent_sem.at[2])
    take(two_code.at[0], sent_sem.at[3])
    take(z_code.at[0], sent_sem.at[4])
    take(whole.at[0, 0, 0], sent_sem.at[5])
    take(whole.at[0, pl.ds(0, 3), pl.ds(0, 2)], sent_sem.at[6])
    take(whole.at[pl.ds(0, 3), pl.ds(0, 2)], sent_sem.at[7])
    take(whole.at[pl.ds(0, 2)], sent_sem.at[8])
    take(whole.at[pl.ds(0, 2)], twin_sem.at[0])


def hand_on(whole, first, second, out, first_out, second_out, sems):
    step = whole.shape[0] // PIECES
    copies = [
        pltpu.make_async_copy(first, first_out, sems.at[PIECES]),
        pltpu.make_async_copy(second, second_out, sems.at[PIECES + 1]),
    ]
    for i in range(PIECES):
        rows = pl.ds(i * step, step)
        copies.append(pltpu.make_async_copy(whole.at[rows, :], out.at[rows, :], sems.at[i]))
    for copy in copies:
        copy.start()
    for copy in copies:
        copy.wait()


def shards(activations, cotangent, tile_rows, params, first_moment, second_moment):
    rows, depth = activations.shape
    count = depth // BLOCK
    bf16, i16 = jnp.bfloat16, jnp.int16
    anywhere = pl.BlockSpec(memory_space=pltpu.HBM)
    vmem = pl.BlockSpec(memory_space=pltpu.VMEM)
    dma = pltpu.SemaphoreType.DMA
    whole, first_new, second_new = pl.pallas_call(
        kernel,
        out_shape=(
            pltpu.VMEM((count, SIDE, SIDE, ROWS, COLS), bf16),
            pltpu.VMEM((ROWS, COLS), F32),
            pltpu.VMEM((ROWS, COLS), F32),
        ),
        in_specs=[
            anywhere, anywhere, anywhere, anywhere, anywhere, anywhere,
        ],
        out_specs=(vmem, vmem, vmem),
        scratch_shapes=[
            pltpu.VMEM((4, rows, BLOCK), bf16),
            pltpu.VMEM((rows, COLS), bf16),
            pltpu.SMEM(tile_rows.shape, jnp.int32),
            pltpu.VMEM((ROWS, COLS), bf16),
            pltpu.VMEM((2, ROWS, COLS), F32),
            pltpu.VMEM((2, 2, SIDE, SIDE, ROWS, COLS), F32),
            pltpu.VMEM((2, SIDE, SIDE, ROWS, COLS), F32),
            pltpu.VMEM((2, 2, ROWS, HALF), F32),
            pltpu.VMEM((2, 2, 2, 3, SIDE, ROWS, HALF), i16),
            pltpu.VMEM((2, 2, 2, 3, ROWS, HALF), i16),
            pltpu.VMEM((2, 2, ROWS, HALF), i16),
            pltpu.VMEM((2, 26, 8, LANES), F32),
            pltpu.VMEM((1200, LANES), i16),
            dma((9,)),
            dma((9,)),
            dma((2,)),
            dma((2, 2)),
            dma((2, 2)),
            dma((2,)),
            dma((2,)),
            dma((2, 2, 3)),
            dma((2, 2, 3, 2)),
            dma((1,)),
        ],
        compiler_params=pltpu.CompilerParams(
            collective_id=0, has_side_effects=True, vmem_limit_bytes=58 * 2**20
        ),
    )(activations, cotangent, tile_rows, params, first_moment, second_moment)
    whole = whole.reshape(depth, COLS)
    return pl.pallas_call(
        hand_on,
        out_shape=tuple(jax.ShapeDtypeStruct(a.shape, a.dtype) for a in (whole, first_new, second_new)),
        in_specs=[pl.BlockSpec(memory_space=pl.ANY)] * 3,
        out_specs=(anywhere,) * 3,
        scratch_shapes=[dma((PIECES + 2,))],
        compiler_params=pltpu.CompilerParams(vmem_limit_bytes=4 * 2**20),
    )(whole, first_new, second_new)


def solution(mesh):
    in_specs = (
        P(("exp", "inner", "outer"), None),
        P(("exp", "inner", "outer"), None),
        P(("exp", "inner", "outer")),
        P(("exp", "inner"), None),
        P(("exp", "inner"), None),
        P(("exp", "inner"), None),
    )
    out_specs = (
        P("exp", None),
        P(("exp", "inner", "outer"), None),
        P(("exp", "inner", "outer"), None),
    )
    return jax.shard_map(shards, mesh=mesh, in_specs=in_specs, out_specs=out_specs, check_vma=False)
```
